32 devices in a mesh: rep: 4 (over y, x), fsdp: 8 (over z, core).
Axes of the slice: x: 2, y: 2, z: 4, core: 2. Of those that a mesh axis runs over, the one named last changes fastest.
Arguments:
- pseudo_grad: float32 [4, 4096, 256], P('rep', 'fsdp'), may hold values from -6 to 6
- error_buf: float32 [4, 4096, 256], P('rep', 'fsdp'), may hold values from -6 to 6
- momentum: float32 [4096, 256], P('fsdp'), may hold values from -4 to 4
- params: float32 [4096, 256], P('fsdp'), may hold values from -6 to 6
- picks: int32 [4, 64], P('rep', 'fsdp'), may hold values from 0 to 511, as said below
Outputs:
- new_params: float32 [4096, 256], P('fsdp')
- new_momentum: float32 [4096, 256], P('fsdp')
- new_error: float32 [4, 4096, 256], P('rep', 'fsdp')
- gathered: bfloat16 [4096, 256], replicated
The draws below stay inside these ranges and needn't reach their ends.
Inputs may be any that keep to these rules, and one draw needn't show every extreme that they name: `picks`: entries j of a row with the same j // 8 are distinct.
All inputs are finite; a program needn't handle non-finite values.
Results may differ from the reference program's by a relative error of at most 0.0017.
Values may be sent and summed in bfloat16 or wider, within the bound.
A program may use at most 64 MiB of HBM per device.

```python
import jax
import jax.numpy as jnp

BLOCK = 256
BLOCKS_DEV = 512
TOPK = 8
REPLICAS = 4
BLOCKS = 4096
TOPK_ALL = 64
N_FSDP = 8


def draw_picks(key, part):
    key = jax.random.fold_in(key, 11)
    shard_count = REPLICAS * N_FSDP
    keys = jax.random.split(key, shard_count)
    inner = jax.vmap(lambda single: 1 + jax.random.permutation(single, BLOCKS_DEV - 2)[:TOPK])(keys)
    special = jax.random.randint(jax.random.fold_in(key, 1), (), 0, shard_count)
    forced = (jnp.arange(shard_count) == special)[:, None]
    column = jnp.arange(TOPK)[None, :]
    inner = jnp.where(forced & (column == 0), BLOCKS_DEV - 1, inner)
    inner = jnp.where(forced & (column == 1), 0, inner)
    return inner.reshape(REPLICAS, TOPK_ALL).astype(jnp.int32)


def shard_levels(stream_key, extent, shards, least, high):
    factor_of = 1.0
    for axis_at, shards_of in shards:
        steps = jax.random.uniform(jax.random.fold_in(jax.random.fold_in(stream_key, 6), axis_at), (shards_of,), jnp.float32, least / len(shards), high / len(shards))
        factor_of = factor_of * jnp.repeat(jnp.exp(steps), extent[axis_at] // shards_of).reshape((-1,) + (1,) * (len(extent) - 1 - axis_at))
    return factor_of


def noise(own_key, shape, scale, most, shards=(), kind=jnp.bfloat16):
    level = shard_levels(own_key, shape, shards, -0.22, 0.18) if shards else 1.0
    array = jax.random.normal(own_key, shape, jnp.float32) * scale * level
    return jnp.minimum(jnp.maximum(array, -most), most).astype(kind)


def setup_inputs(seed: int = 0) -> dict:
    splits = jax.random.split(jax.random.key(seed), 6)
    pseudo_grad = noise(splits[0], (REPLICAS, BLOCKS, BLOCK), 1.0, 6.0, ((0, 4), (1, 8)), jnp.float32)
    error_buf = noise(splits[1], (REPLICAS, BLOCKS, BLOCK), 1.0, 6.0, ((0, 4), (1, 8)), jnp.float32)
    momentum = noise(splits[2], (BLOCKS, BLOCK), 0.5, 4.0, ((0, 8),), jnp.float32)
    params = noise(splits[3], (BLOCKS, BLOCK), 1.0, 6.0, ((0, 8),), jnp.float32)
    picks = draw_picks(jax.random.fold_in(splits[5], 71), 0)
    return dict(pseudo_grad=pseudo_grad, error_buf=error_buf, momentum=momentum, params=params, picks=picks)


def reference(pseudo_grad, error_buf, momentum, params, picks):
    accumulated = 0.95 * error_buf + pseudo_grad
    owners = (jnp.arange(TOPK_ALL, dtype=jnp.int32) // TOPK) * BLOCKS_DEV
    global_picks = picks + owners[None, :]
    positions = jnp.arange(BLOCKS, dtype=jnp.int32)
    chosen = jnp.any(global_picks[:, :, None] == positions[None, None, :], axis=1).astype(jnp.float32)
    kept = accumulated * chosen[:, :, None]
    new_error = accumulated - kept
    delta = jnp.sum(kept, axis=0) / REPLICAS
    new_momentum = 0.9 * momentum + delta
    new_params = params - 0.7 * (delta + 0.9 * new_momentum)
    gathered = new_params.astype(jnp.bfloat16)
    return new_params, new_momentum, new_error, gathered
```

```python
import functools

import jax
import jax.numpy as jnp
from jax import lax
from jax.experimental import pallas as pl
from jax.experimental.pallas import tpu as pltpu
from jax.sharding import PartitionSpec as P

DECAY_RATE = 0.95
MOMENTUM_COEF = 0.9
STEP_SCALE = 0.7
MESH = pl.DeviceIdType.MESH


def exchange_kernel(
    replicas, shards, topk, picks_hbm, grad_hbm, error_hbm, momentum_hbm, params_hbm,
    params_out, momentum_out, error_out, gathered,
    picks_ref, grad, error, momentum, params, payload,
    in_sem, pay_send, pay_recv, z_send, z_recv, plane_send, plane_recv, core_send, core_recv,
):
    rep, fsdp = lax.axis_index("rep"), lax.axis_index("fsdp")
    groups = shards // 2
    group, core = fsdp // 2, fsdp % 2
    rows, width = grad.shape
    part = rows // replicas

    def mate(offset):
        return (lax.rem(rep + offset, replicas), fsdp)

    def along(offset):
        return (rep, lax.rem(group + offset, groups) * 2 + core)

    sibling = (rep, group * 2 + 1 - core)

    def remote(src, dst, send, recv, device):
        return pltpu.make_async_remote_copy(
            src_ref=src, dst_ref=dst, send_sem=send, recv_sem=recv, device_id=device, device_id_type=MESH
        )

    barrier = pltpu.get_barrier_semaphore()
    partners = [mate(m) for m in range(1, replicas)] + [along(d) for d in range(1, groups)] + [sibling]
    for device in partners:
        pl.semaphore_signal(barrier, inc=1, device_id=device, device_id_type=MESH)

    loads = [
        pltpu.make_async_copy(src, dst, in_sem.at[i])
        for i, (src, dst) in enumerate(
            ((grad_hbm.at[0], grad), (error_hbm.at[0], error), (momentum_hbm, momentum),
             (params_hbm, params), (picks_hbm, picks_ref))
        )
    ]
    loads[4].start()
    for load in loads[:4]:
        load.start()
    loads[4].wait()
    loads[0].wait()
    loads[1].wait()

    for j in range(topk):
        pick = picks_ref[0, j]
        payload[0, j, :] = DECAY_RATE * error[pick, :] + grad[pick, :]
        payload[0, topk + j, :] = jnp.full((width,), pick.astype(jnp.float32))
    pl.semaphore_wait(barrier, len(partners))
    pays = [
        remote(payload.at[0], payload.at[m], pay_send.at[m], pay_recv.at[m], mate(m)) for m in range(1, replicas)
    ]
    for pay in pays:
        pay.start()

    positions = lax.broadcasted_iota(jnp.int32, (rows, width), 0)
    hit = positions == picks_ref[0, 0]
    for j in range(1, topk):
        hit = jnp.logical_or(hit, positions == picks_ref[0, j])
    error_out[...] = jnp.where(hit, 0.0, DECAY_RATE * error[...] + grad[...])
    loads[2].wait()
    loads[3].wait()

    lanes = lax.broadcasted_iota(jnp.int32, (topk, rows), 1).astype(jnp.float32)
    for pay in pays:
        pay.wait_recv()
    spread = jnp.concatenate(
        [(payload[m, topk : 2 * topk, 0:1] == lanes).astype(jnp.float32) for m in range(replicas)], axis=0
    )
    values = jnp.concatenate([payload[m, :topk, :] for m in range(replicas)], axis=0)
    summed = lax.dot_general(
        spread, values, (((0,), (0,)), ((), ())),
        precision=lax.Precision.HIGHEST, preferred_element_type=jnp.float32,
    )
    delta = summed / replicas
    new_momentum = MOMENTUM_COEF * momentum[...] + delta
    new_params = params[...] - STEP_SCALE * (delta + MOMENTUM_COEF * new_momentum)
    own_rows = pl.ds(pl.multiple_of(fsdp * rows, rows), rows)
    gathered[own_rows, :] = new_params.astype(jnp.bfloat16)

    def piece(g, c, s):
        return gathered.at[pl.ds(pl.multiple_of((g * 2 + c) * rows + s * part, part), part), :]

    sends = []

    def go(copy):
        copy.start()
        sends.append(copy)
        return copy

    outs = []
    for d in range(1, groups):
        own = piece(group, core, rep)
        outs.append(go(remote(own, own, z_send.at[d], z_recv.at[d], along(d))))
    whole = gathered.at[own_rows, :]
    siblings = [go(remote(whole, whole, core_send.at[0, 0], core_recv.at[0, 0], sibling))]
    params_out[...] = new_params
    momentum_out[...] = new_momentum

    planes = {}
    for d in range(1, groups):
        outs[d - 1].wait_recv()
        source = lax.rem(group + groups - d, groups)
        got = piece(source, core, rep)
        for m in range(1, replicas):
            planes[d, m] = go(remote(got, got, plane_send.at[d, m], plane_recv.at[d, m], mate(m)))
        siblings.append(go(remote(got, got, core_send.at[d, 0], core_recv.at[d, 0], sibling)))
    for d in range(1, groups):
        source = lax.rem(group + groups - d, groups)
        for m in range(1, replicas):
            planes[d, m].wait_recv()
            got = piece(source, core, lax.rem(rep + replicas - m, replicas))
            siblings.append(go(remote(got, got, core_send.at[d, m], core_recv.at[d, m], sibling)))
    for copy in siblings:
        copy.wait_recv()
    for pay in pays:
        pay.wait_send()
    for copy in sends:
        copy.wait_send()


def write_kernel(params, momentum, error, gathered, params_out, momentum_out, error_out, gathered_out, sem):
    pairs = ((gathered, gathered_out), (params, params_out), (momentum, momentum_out), (error, error_out.at[0]))
    copies = [pltpu.make_async_copy(src, dst, sem.at[i]) for i, (src, dst) in enumerate(pairs)]
    for copy in copies:
        copy.start()
    for copy in copies:
        copy.wait()


def per_device(replicas, shards, pseudo_grad, error_buf, momentum, params, picks):
    rows, width = params.shape
    topk = picks.shape[1]
    groups = shards // 2
    f32, bf16 = jnp.float32, jnp.bfloat16
    shard = (rows, width)
    dma = pltpu.SemaphoreType.DMA
    vmem = pl.BlockSpec(memory_space=pltpu.VMEM)
    hbm = pl.BlockSpec(memory_space=pltpu.HBM)
    held = pl.pallas_call(
        functools.partial(exchange_kernel, replicas, shards, topk),
        out_shape=(
            pltpu.VMEM(shard, f32),
            pltpu.VMEM(shard, f32),
            pltpu.VMEM(shard, f32),
            pltpu.VMEM((shards * rows, width), bf16),
        ),
        in_specs=[hbm] * 5,
        out_specs=[vmem] * 4,
        scratch_shapes=[
            pltpu.SMEM((1, topk), jnp.int32),
            pltpu.VMEM(shard, f32),
            pltpu.VMEM(shard, f32),
            pltpu.VMEM(shard, f32),
            pltpu.VMEM(shard, f32),
            pltpu.VMEM((replicas, 2 * topk, width), f32),
            dma((5,)),
            dma((replicas,)),
            dma((replicas,)),
            dma((groups,)),
            dma((groups,)),
            dma((groups, replicas)),
            dma((groups, replicas)),
            dma((groups, replicas)),
            dma((groups, replicas)),
        ],
        compiler_params=pltpu.CompilerParams(
            collective_id=0, has_side_effects=True, vmem_limit_bytes=32 * 1024 * 1024
        ),
        name="exchange",
    )(*(pltpu.with_memory_space_constraint(x, pltpu.HBM) for x in (picks, pseudo_grad, error_buf, momentum, params)))
    return pl.pallas_call(
        write_kernel,
        out_shape=(
            jax.ShapeDtypeStruct(shard, f32),
            jax.ShapeDtypeStruct(shard, f32),
            jax.ShapeDtypeStruct((1, rows, width), f32),
            jax.ShapeDtypeStruct((shards * rows, width), bf16),
        ),
        in_specs=[vmem] * 4,
        out_specs=[hbm] * 4,
        scratch_shapes=[dma((4,))],
        name="write_out",
    )(*held)


def solution(mesh):
    in_specs = (
        P("rep", "fsdp", None),
        P("rep", "fsdp", None),
        P("fsdp", None),
        P("fsdp", None),
        P("rep", "fsdp"),
    )
    out_specs = (P("fsdp", None), P("fsdp", None), P("rep", "fsdp", None), P())
    step = functools.partial(per_device, mesh.shape["rep"], mesh.shape["fsdp"])
    return jax.shard_map(step, mesh=mesh, in_specs=in_specs, out_specs=out_specs, check_vma=False)
```

```python
import functools

import jax
import jax.numpy as jnp
from jax import lax
from jax.experimental import pallas as pl
from jax.experimental.pallas import tpu as pltpu
from jax.sharding import PartitionSpec as P

DECAY_RATE = 0.95
MOMENTUM_COEF = 0.9
STEP_SCALE = 0.7
MESH = pl.DeviceIdType.MESH


def exchange_kernel(
    replicas, shards, topk, picks_hbm, grad_hbm, error_hbm, momentum_hbm, params_hbm,
    params_out, momentum_out, error_out, gathered,
    picks_ref, grad, error, momentum, params, payload,
    in_sem, pay_send, pay_recv, z_send, z_recv, plane_send, plane_recv, core_send, core_recv,
):
    rep, fsdp = lax.axis_index("rep"), lax.axis_index("fsdp")
    groups = shards // 2
    group, core = fsdp // 2, fsdp % 2
    rows, width = grad.shape
    part = rows // replicas

    def mate(offset):
        return (lax.rem(rep + offset, replicas), fsdp)

    def along(offset):
        return (rep, lax.rem(group + offset, groups) * 2 + core)

    sibling = (rep, group * 2 + 1 - core)

    def remote(src, dst, send, recv, device):
        return pltpu.make_async_remote_copy(
            src_ref=src, dst_ref=dst, send_sem=send, recv_sem=recv, device_id=device, device_id_type=MESH
        )

    barrier = pltpu.get_barrier_semaphore()
    partners = [mate(m) for m in range(1, replicas)] + [along(d) for d in range(1, groups)] + [sibling]
    for device in partners:
        pl.semaphore_signal(barrier, inc=1, device_id=device, device_id_type=MESH)

    loads = [
        pltpu.make_async_copy(src, dst, in_sem.at[i])
        for i, (src, dst) in enumerate(
            ((grad_hbm.at[0], grad), (error_hbm.at[0], error), (momentum_hbm, momentum),
             (params_hbm, params), (picks_hbm, picks_ref))
        )
    ]
    loads[4].start()
    for load in loads[:4]:
        load.start()
    loads[4].wait()
    loads[0].wait()
    loads[1].wait()

    lane = lax.broadcasted_iota(jnp.int32, (1, width), 1)
    numbers = jnp.zeros((1, width), jnp.float32)
    for j in range(topk):
        pick = picks_ref[0, j]
        payload[rep, j, :] = DECAY_RATE * error[pick, :] + grad[pick, :]
        numbers = jnp.where(lane == rep * topk + j, (pick + 1).astype(jnp.float32), numbers)
    payload[rep, topk : 2 * topk, :] = jnp.broadcast_to(numbers, (topk, width))
    pl.semaphore_wait(barrier, len(partners))
    own_pay = payload.at[rep]
    pays = [remote(own_pay, own_pay, pay_send.at[m], pay_recv.at[m], mate(m)) for m in range(1, replicas)]
    for pay in pays:
        pay.start()

    positions = lax.broadcasted_iota(jnp.int32, (rows, width), 0)
    hit = positions == picks_ref[0, 0]
    for j in range(1, topk):
        hit = jnp.logical_or(hit, positions == picks_ref[0, j])
    error_out[...] = jnp.where(hit, 0.0, DECAY_RATE * error[...] + grad[...])
    loads[2].wait()
    loads[3].wait()

    for pay in pays:
        pay.wait_recv()
    named = sum(payload[m, topk : topk + 1, :] for m in range(replicas))
    values = jnp.concatenate([payload[m, :topk, :] for m in range(replicas)], axis=0)
    parts, rest = [], values
    for _ in range(3):
        parts.append(rest.astype(jnp.bfloat16))
        rest = rest - parts[-1].astype(jnp.float32)
    places = (lax.broadcasted_iota(jnp.int32, (part, width), 0) + 1).astype(jnp.float32)

    def update(s):
        here = pl.ds(pl.multiple_of(s * part, part), part)
        spread = (places + (s * part).astype(jnp.float32) == named).astype(jnp.float32)
        spread = spread[:, : replicas * topk].astype(jnp.bfloat16)
        summed = sum(jnp.dot(spread, piece, preferred_element_type=jnp.float32) for piece in reversed(parts))
        delta = summed / replicas
        new_momentum = MOMENTUM_COEF * momentum[here, :] + delta
        new_params = params[here, :] - STEP_SCALE * (delta + MOMENTUM_COEF * new_momentum)
        gathered[pl.ds(pl.multiple_of(fsdp * rows + s * part, part), part), :] = new_params.astype(jnp.bfloat16)
        params_out[here, :] = new_params
        momentum_out[here, :] = new_momentum

    def piece(g, s, start=0, count=part):
        first = (g * 2 + core) * rows + s * part + start
        return gathered.at[pl.ds(pl.multiple_of(first, count), count), :]

    sends, siblings = [], []

    def go(copy):
        copy.start()
        sends.append(copy)
        return copy

    def share(ref, at):
        siblings.append(go(remote(ref, ref, core_send.at[at], core_recv.at[at], sibling)))

    update(rep)
    own = piece(group, rep)
    outs = [go(remote(own, own, z_send.at[d], z_recv.at[d], along(d))) for d in range(1, groups)]
    for m in range(1, replicas):
        update(lax.rem(rep + m, replicas))
    whole = gathered.at[pl.ds(pl.multiple_of(fsdp * rows, rows), rows), :]
    share(whole, (0, 0))

    x, y = rep % 2, rep // 2
    lines = replicas // 2
    half = part // 2
    across = (y * 2 + 1 - x, fsdp)

    def line(offset):
        return lax.rem(y + offset, lines)

    def source(d):
        return lax.rem(group + groups - d, groups)

    def z_stage(d):
        outs[d - 1].wait_recv()
        got = piece(source(d), rep)
        copies[d] = [go(remote(got, got, plane_send.at[d, 0], plane_recv.at[d, 0], across))]
        for m in range(1, lines):
            to = (line(m) * 2 + x, fsdp)
            copies[d].append(go(remote(got, got, plane_send.at[d, m], plane_recv.at[d, m], to)))
        share(got, (d, 0))

    def plane_stage(d):
        firsts[d], seconds[d] = [], []
        copies[d][0].wait_recv()
        got = piece(source(d), y * 2 + 1 - x)
        first = piece(source(d), y * 2 + 1 - x, 0, half)
        for m in range(1, lines):
            at = lines + m
            to = (line(m) * 2 + x, fsdp)
            firsts[d].append(go(remote(first, first, plane_send.at[d, at], plane_recv.at[d, at], to)))
        share(got, (d, 1))
        for m in range(1, lines):
            copies[d][m].wait_recv()
            s = line(lines - m) * 2 + x
            second = piece(source(d), s, half, half)
            at = 2 * lines + m
            seconds[d].append(go(remote(second, second, plane_send.at[d, at], plane_recv.at[d, at], across)))
            share(piece(source(d), s), (d, 1 + m))

    def last_stage(d):
        for m in range(1, lines):
            s = line(lines - m) * 2 + 1 - x
            firsts[d][m - 1].wait_recv()
            seconds[d][m - 1].wait_recv()
            share(piece(source(d), s), (d, lines + m))

    copies, firsts, seconds = {}, {}, {}
    for turn in range(1, groups + 2):
        for stage, late in ((z_stage, 0), (plane_stage, 1), (last_stage, 2)):
            if 1 <= turn - late < groups:
                stage(turn - late)
    for copy in siblings:
        copy.wait_recv()
    for pay in pays:
        pay.wait_send()
    for copy in sends:
        copy.wait_send()


def write_kernel(params, momentum, error, gathered, params_out, momentum_out, error_out, gathered_out, sem):
    pairs = ((gathered, gathered_out), (params, params_out), (momentum, momentum_out), (error, error_out.at[0]))
    copies = [pltpu.make_async_copy(src, dst, sem.at[i]) for i, (src, dst) in enumerate(pairs)]
    for copy in copies:
        copy.start()
    for copy in copies:
        copy.wait()


def per_device(replicas, shards, pseudo_grad, error_buf, momentum, params, picks):
    rows, width = params.shape
    topk = picks.shape[1]
    groups = shards // 2
    f32, bf16 = jnp.float32, jnp.bfloat16
    shard = (rows, width)
    dma = pltpu.SemaphoreType.DMA
    vmem = pl.BlockSpec(memory_space=pltpu.VMEM)
    hbm = pl.BlockSpec(memory_space=pltpu.HBM)
    held = pl.pallas_call(
        functools.partial(exchange_kernel, replicas, shards, topk),
        out_shape=(
            pltpu.VMEM(shard, f32),
            pltpu.VMEM(shard, f32),
            pltpu.VMEM(shard, f32),
            pltpu.VMEM((shards * rows, width), bf16),
        ),
        in_specs=[hbm] * 5,
        out_specs=[vmem] * 4,
        scratch_shapes=[
            pltpu.SMEM((1, topk), jnp.int32),
            pltpu.VMEM(shard, f32),
            pltpu.VMEM(shard, f32),
            pltpu.VMEM(shard, f32),
            pltpu.VMEM(shard, f32),
            pltpu.VMEM((replicas, 2 * topk, width), f32),
            dma((5,)),
            dma((replicas,)),
            dma((replicas,)),
            dma((groups,)),
            dma((groups,)),
            dma((groups, 3 * replicas // 2)),
            dma((groups, 3 * replicas // 2)),
            dma((groups, replicas)),
            dma((groups, replicas)),
        ],
        compiler_params=pltpu.CompilerParams(
            collective_id=0, has_side_effects=True, vmem_limit_bytes=32 * 1024 * 1024
        ),
        name="exchange",
    )(*(pltpu.with_memory_space_constraint(x, pltpu.HBM) for x in (picks, pseudo_grad, error_buf, momentum, params)))
    return pl.pallas_call(
        write_kernel,
        out_shape=(
            jax.ShapeDtypeStruct(shard, f32),
            jax.ShapeDtypeStruct(shard, f32),
            jax.ShapeDtypeStruct((1, rows, width), f32),
            jax.ShapeDtypeStruct((shards * rows, width), bf16),
        ),
        in_specs=[vmem] * 4,
        out_specs=[hbm] * 4,
        scratch_shapes=[dma((4,))],
        compiler_params=pltpu.CompilerParams(vmem_limit_bytes=16 * 1024 * 1024),
        name="write_out",
    )(*(pltpu.with_memory_space_constraint(x, pltpu.VMEM) for x in held))


def solution(mesh):
    in_specs = (
        P("rep", "fsdp", None),
        P("rep", "fsdp", None),
        P("fsdp", None),
        P("fsdp", None),
        P("rep", "fsdp"),
    )
    out_specs = (P("fsdp", None), P("fsdp", None), P("rep", "fsdp", None), P())
    step = functools.partial(per_device, mesh.shape["rep"], mesh.shape["fsdp"])
    return jax.shard_map(step, mesh=mesh, in_specs=in_specs, out_specs=out_specs, check_vma=False)
```

```python
import functools

import jax
import jax.numpy as jnp
from jax import lax
from jax.experimental import pallas as pl
from jax.experimental.pallas import tpu as pltpu
from jax.sharding import PartitionSpec as P

DECAY_RATE = 0.95
MOMENTUM_COEF = 0.9
STEP_SCALE = 0.7
MESH = pl.DeviceIdType.MESH


def exchange_kernel(
    replicas, shards, topk, picks_hbm, grad_hbm, error_hbm, momentum_hbm, params_hbm,
    params_out, momentum_out, error_out, final,
    picks_ref, grad, error, momentum, params, payload, gathered, fixes,
    in_sem, pay_send, pay_recv, z_send, z_recv, plane_send, plane_recv, core_send, core_recv,
    fix_send, fix_recv, fix_core_send, fix_core_recv,
):
    rep, fsdp = lax.axis_index("rep"), lax.axis_index("fsdp")
    groups = shards // 2
    group, core = fsdp // 2, fsdp % 2
    rows, width = grad.shape
    part = rows // replicas
    named_rows = replicas * topk
    f32, bf16 = jnp.float32, jnp.bfloat16

    def mate(offset):
        return (lax.rem(rep + offset, replicas), fsdp)

    def along(offset):
        return (rep, lax.rem(group + offset, groups) * 2 + core)

    sibling = (rep, group * 2 + 1 - core)

    def remote(src, dst, send, recv, device):
        return pltpu.make_async_remote_copy(
            src_ref=src, dst_ref=dst, send_sem=send, recv_sem=recv, device_id=device, device_id_type=MESH
        )

    barrier = pltpu.get_barrier_semaphore()
    partners = [mate(m) for m in range(1, replicas)] + [along(d) for d in range(1, groups)] + [sibling]
    for device in partners:
        pl.semaphore_signal(barrier, inc=1, device_id=device, device_id_type=MESH)

    loads = [
        pltpu.make_async_copy(src, dst, in_sem.at[i])
        for i, (src, dst) in enumerate(
            ((picks_hbm, picks_ref), (momentum_hbm, momentum), (params_hbm, params),
             (grad_hbm.at[0], grad), (error_hbm.at[0], error))
        )
    ]
    for load in loads:
        load.start()
    for load in loads[:3]:
        load.wait()

    def step(moment, weight, delta):
        new_momentum = MOMENTUM_COEF * moment + delta
        return new_momentum, weight - STEP_SCALE * (delta + MOMENTUM_COEF * new_momentum)

    own_rows = pl.ds(pl.multiple_of(fsdp * rows, rows), rows)
    gathered[own_rows, :] = step(momentum[...], params[...], 0.0)[1].astype(bf16)

    loads[3].wait()
    loads[4].wait()
    lane = lax.broadcasted_iota(jnp.int32, (1, width), 1)
    numbers = jnp.zeros((1, width), f32)
    for j in range(topk):
        pick = picks_ref[0, j]
        payload[rep, j, :] = DECAY_RATE * error[pick, :] + grad[pick, :]
        numbers = jnp.where(lane == rep * topk + j, (pick + 1).astype(f32), numbers)
    payload[rep, topk : 2 * topk, :] = jnp.broadcast_to(numbers, (topk, width))
    pl.semaphore_wait(barrier, len(partners))

    def piece(g, s):
        return gathered.at[pl.ds(pl.multiple_of((g * 2 + core) * rows + s * part, part), part), :]

    def source(d):
        return lax.rem(group + groups - d, groups)

    sends, siblings, planes = [], {}, {}

    def go(copy):
        copy.start()
        sends.append(copy)
        return copy

    def share(ref, d, m):
        siblings[d, m] = go(remote(ref, ref, core_send.at[d, m], core_recv.at[d, m], sibling))

    own_pay = payload.at[rep]
    pays = [go(remote(own_pay, own_pay, pay_send.at[m], pay_recv.at[m], mate(m))) for m in range(1, replicas)]
    own = piece(group, rep)
    outs = [go(remote(own, own, z_send.at[d], z_recv.at[d], along(d))) for d in range(1, groups)]
    share(gathered.at[own_rows, :], 0, 0)

    positions = lax.broadcasted_iota(jnp.int32, (rows, width), 0)
    hit = positions == picks_ref[0, 0]
    for j in range(1, topk):
        hit = jnp.logical_or(hit, positions == picks_ref[0, j])
    error_out[...] = jnp.where(hit, 0.0, DECAY_RATE * error[...] + grad[...])

    def z_stage(d):
        outs[d - 1].wait_recv()
        got = piece(source(d), rep)
        for m in range(1, replicas):
            planes[d, m] = go(remote(got, got, plane_send.at[d, m], plane_recv.at[d, m], mate(m)))
        share(got, d, 0)

    places = (positions + 1).astype(f32)

    def spread_of(named):
        return (places == named).astype(f32)[:, :named_rows].astype(bf16)

    def own_stage():
        for pay in pays:
            pay.wait_recv()
        named = sum(payload[m, topk : topk + 1, :] for m in range(replicas))
        spread = spread_of(named)
        rest = jnp.concatenate([payload[m, :topk, :] for m in range(replicas)], axis=0)
        summed = 0.0
        for _ in range(3):
            top = rest.astype(bf16)
            summed = summed + jnp.dot(spread, top, preferred_element_type=f32)
            rest = rest - top.astype(f32)
        new_momentum, new_params = step(momentum[...], params[...], summed / replicas)
        rounded = new_params.astype(bf16)
        picked = lax.dot_general(spread, rounded, (((0,), (0,)), ((), ())), preferred_element_type=f32)
        fixes[fsdp, :named_rows, :] = picked.astype(bf16)
        high = jnp.floor(named / 16)
        row = lax.broadcasted_iota(jnp.int32, (16, width), 0)
        digits = jnp.where(row == 0, high, jnp.where(row == 1, named - 16 * high, 0.0))
        fixes[fsdp, named_rows:, :] = digits.astype(bf16)
        fix = fixes.at[fsdp]
        for d in range(1, groups):
            fix_outs.append(go(remote(fix, fix, fix_send.at[d], fix_recv.at[d], along(d))))
        fix_siblings.append(go(remote(fix, fix, fix_core_send.at[0], fix_core_recv.at[0], sibling)))
        params_out[...] = new_params
        momentum_out[...] = new_momentum
        final[own_rows, :] = rounded

    def fix_shard(shard):
        here = pl.ds(pl.multiple_of(shard * rows, rows), rows)
        digits = fixes[shard, named_rows:, :].astype(f32)
        spread = spread_of(16 * digits[0:1, :] + digits[1:2, :])
        total = jnp.dot(spread, fixes[shard, :named_rows, :], preferred_element_type=f32)
        count = jnp.dot(spread, jnp.ones((named_rows, width), bf16), preferred_element_type=f32)
        value = total / jnp.maximum(count, 1.0)
        final[here, :] = jnp.where(count > 0.5, value, gathered[here, :].astype(f32)).astype(bf16)

    fix_outs, fix_siblings = [], []
    z_stage(1)
    own_stage()
    for d in range(2, groups):
        z_stage(d)
    for d in range(1, groups):
        fix_outs[d - 1].wait_recv()
        fix = fixes.at[source(d) * 2 + core]
        fix_siblings.append(go(remote(fix, fix, fix_core_send.at[d], fix_core_recv.at[d], sibling)))
        for m in range(1, replicas):
            planes[d, m].wait_recv()
            share(piece(source(d), lax.rem(rep + replicas - m, replicas)), d, m)
    for d in range(1, groups):
        fix_shard(source(d) * 2 + core)
    for d in range(groups):
        fix_siblings[d].wait_recv()
        for m in range(replicas if d else 1):
            siblings[d, m].wait_recv()
        fix_shard(source(d) * 2 + 1 - core)
    for copy in sends:
        copy.wait_send()


def write_kernel(params, momentum, error, gathered, params_out, momentum_out, error_out, gathered_out, sem):
    pairs = ((gathered, gathered_out), (params, params_out), (momentum, momentum_out), (error, error_out.at[0]))
    copies = [pltpu.make_async_copy(src, dst, sem.at[i]) for i, (src, dst) in enumerate(pairs)]
    for copy in copies:
        copy.start()
    for copy in copies:
        copy.wait()


def per_device(replicas, shards, pseudo_grad, error_buf, momentum, params, picks):
    rows, width = params.shape
    topk = picks.shape[1]
    groups = shards // 2
    f32, bf16 = jnp.float32, jnp.bfloat16
    shard = (rows, width)
    dma = pltpu.SemaphoreType.DMA
    vmem = pl.BlockSpec(memory_space=pltpu.VMEM)
    hbm = pl.BlockSpec(memory_space=pltpu.HBM)
    held = pl.pallas_call(
        functools.partial(exchange_kernel, replicas, shards, topk),
        out_shape=(
            pltpu.VMEM(shard, f32),
            pltpu.VMEM(shard, f32),
            pltpu.VMEM(shard, f32),
            pltpu.VMEM((shards * rows, width), bf16),
        ),
        in_specs=[hbm] * 5,
        out_specs=[vmem] * 4,
        scratch_shapes=[
            pltpu.SMEM((1, topk), jnp.int32),
            pltpu.VMEM(shard, f32),
            pltpu.VMEM(shard, f32),
            pltpu.VMEM(shard, f32),
            pltpu.VMEM(shard, f32),
            pltpu.VMEM((replicas, 2 * topk, width), f32),
            pltpu.VMEM((shards * rows, width), bf16),
            pltpu.VMEM((shards, replicas * topk + 16, width), bf16),
            dma((5,)),
            dma((replicas,)),
            dma((replicas,)),
            dma((groups,)),
            dma((groups,)),
            dma((groups, replicas)),
            dma((groups, replicas)),
            dma((groups, replicas)),
            dma((groups, replicas)),
            dma((groups,)),
            dma((groups,)),
            dma((groups,)),
            dma((groups,)),
        ],
        compiler_params=pltpu.CompilerParams(
            collective_id=0, has_side_effects=True, vmem_limit_bytes=32 * 1024 * 1024
        ),
        name="exchange",
    )(*(pltpu.with_memory_space_constraint(x, pltpu.HBM) for x in (picks, pseudo_grad, error_buf, momentum, params)))
    return pl.pallas_call(
        write_kernel,
        out_shape=(
            jax.ShapeDtypeStruct(shard, f32),
            jax.ShapeDtypeStruct(shard, f32),
            jax.ShapeDtypeStruct((1, rows, width), f32),
            jax.ShapeDtypeStruct((shards * rows, width), bf16),
        ),
        in_specs=[vmem] * 4,
        out_specs=[hbm] * 4,
        scratch_shapes=[dma((4,))],
        compiler_params=pltpu.CompilerParams(vmem_limit_bytes=16 * 1024 * 1024),
        name="write_out",
    )(*(pltpu.with_memory_space_constraint(x, pltpu.VMEM) for x in held))


def solution(mesh):
    in_specs = (
        P("rep", "fsdp", None),
        P("rep", "fsdp", None),
        P("fsdp", None),
        P("fsdp", None),
        P("rep", "fsdp"),
    )
    out_specs = (P("fsdp", None), P("fsdp", None), P("rep", "fsdp", None), P())
    step = functools.partial(per_device, mesh.shape["rep"], mesh.shape["fsdp"])
    return jax.shard_map(step, mesh=mesh, in_specs=in_specs, out_specs=out_specs, check_vma=False)
```

```python
import functools

import jax
import jax.numpy as jnp
from jax import lax
from jax.experimental import pallas as pl
from jax.experimental.pallas import tpu as pltpu
from jax.sharding import PartitionSpec as P

DECAY_RATE = 0.95
MOMENTUM_COEF = 0.9
STEP_SCALE = 0.7
MESH = pl.DeviceIdType.MESH


def exchange_kernel(
    replicas, shards, topk, picks_hbm, grad_hbm, error_hbm, momentum_hbm, params_hbm,
    params_out, momentum_out, error_out, final,
    picks_ref, grad, error, momentum, params, payload, gathered, fixes,
    in_sem, pay_send, pay_recv, z_send, z_recv, plane_send, plane_recv, core_send, core_recv,
    fix_send, fix_recv, fix_core_send, fix_core_recv,
):
    rep, fsdp = lax.axis_index("rep"), lax.axis_index("fsdp")
    groups = shards // 2
    group, core = fsdp // 2, fsdp % 2
    rows, width = grad.shape
    part = rows // replicas
    named_rows = replicas * topk
    f32, bf16 = jnp.float32, jnp.bfloat16

    def mate(offset):
        return (lax.rem(rep + offset, replicas), fsdp)

    def along(offset):
        return (rep, lax.rem(group + offset, groups) * 2 + core)

    sibling = (rep, group * 2 + 1 - core)

    def remote(src, dst, send, recv, device):
        return pltpu.make_async_remote_copy(
            src_ref=src, dst_ref=dst, send_sem=send, recv_sem=recv, device_id=device, device_id_type=MESH
        )

    barrier = pltpu.get_barrier_semaphore()
    partners = [mate(m) for m in range(1, replicas)] + [along(d) for d in range(1, groups)] + [sibling]
    for device in partners:
        pl.semaphore_signal(barrier, inc=1, device_id=device, device_id_type=MESH)

    loads = [
        pltpu.make_async_copy(src, dst, in_sem.at[i])
        for i, (src, dst) in enumerate(
            ((picks_hbm, picks_ref), (momentum_hbm, momentum), (params_hbm, params),
             (grad_hbm.at[0], grad), (error_hbm.at[0], error))
        )
    ]
    for load in loads:
        load.start()
    for load in loads[:3]:
        load.wait()

    def step(moment, weight, delta):
        new_momentum = MOMENTUM_COEF * moment + delta
        return new_momentum, weight - STEP_SCALE * (delta + MOMENTUM_COEF * new_momentum)

    own_rows = pl.ds(pl.multiple_of(fsdp * rows, rows), rows)
    gathered[own_rows, :] = step(momentum[...], params[...], 0.0)[1].astype(bf16)

    def piece(g, s):
        return gathered.at[pl.ds(pl.multiple_of((g * 2 + core) * rows + s * part, part), part), :]

    def source(d):
        return lax.rem(group + groups - d, groups)

    sends = []

    def go(copy):
        copy.start()
        sends.append(copy)
        return copy

    def on_line(g):
        return jnp.logical_and(g >= 0, g < groups)

    def came_from(w, j):
        return group + (j if w else -j)

    def onward(w):
        return group + (-1 if w else 1)

    def hop(w, j):
        ref = piece(came_from(w, j), rep)
        to = (rep, onward(w) * 2 + core)
        return remote(ref, ref, z_send.at[w, j], z_recv.at[w, j], to)

    def arrives(w, j):
        return on_line(came_from(w, j))

    def goes(w, j):
        return jnp.logical_and(arrives(w, j), on_line(onward(w)))

    def plane(w, j, m):
        ref = piece(came_from(w, j), rep)
        return remote(ref, ref, plane_send.at[w, j, m], plane_recv.at[w, j, m], mate(m))

    def pair(w, j, m):
        ref = piece(came_from(w, j), lax.rem(rep + replicas - m, replicas))
        return remote(ref, ref, core_send.at[w, j, m], core_recv.at[w, j, m], sibling)

    hops = [(w, j) for j in range(1, groups) for w in range(2)]
    pl.semaphore_wait(barrier, len(partners))
    for w in range(2):
        pl.when(on_line(onward(w)))(hop(w, 0).start)

    loads[3].wait()
    loads[4].wait()
    lane = lax.broadcasted_iota(jnp.int32, (1, width), 1)
    numbers = jnp.zeros((1, width), f32)
    for j in range(topk):
        pick = picks_ref[0, j]
        payload[rep, j, :] = DECAY_RATE * error[pick, :] + grad[pick, :]
        numbers = jnp.where(lane == rep * topk + j, (pick + 1).astype(f32), numbers)
    payload[rep, topk : 2 * topk, :] = jnp.broadcast_to(numbers, (topk, width))

    own_pay = payload.at[rep]
    pays = [go(remote(own_pay, own_pay, pay_send.at[m], pay_recv.at[m], mate(m))) for m in range(1, replicas)]
    own_whole = gathered.at[own_rows, :]
    whole = go(remote(own_whole, own_whole, core_send.at[0, 0, 0], core_recv.at[0, 0, 0], sibling))

    positions = lax.broadcasted_iota(jnp.int32, (rows, width), 0)
    hit = positions == picks_ref[0, 0]
    for j in range(1, topk):
        hit = jnp.logical_or(hit, positions == picks_ref[0, j])
    error_out[...] = jnp.where(hit, 0.0, DECAY_RATE * error[...] + grad[...])

    def z_stage(w, j):
        @pl.when(arrives(w, j))
        def _():
            hop(w, j - 1).wait_recv()
            if j + 1 < groups:
                pl.when(on_line(onward(w)))(hop(w, j).start)
            for m in range(1, replicas):
                plane(w, j, m).start()
            pair(w, j, 0).start()

    def plane_stage(w, j):
        @pl.when(arrives(w, j))
        def _():
            for m in range(1, replicas):
                plane(w, j, m).wait_recv()
                pair(w, j, m).start()

    def last_stage(w, j):
        @pl.when(arrives(w, j))
        def _():
            for m in range(replicas):
                pair(w, j, m).wait_recv()
            fix_shard(came_from(w, j) * 2 + 1 - core)

    def drain(w, j):
        @pl.when(arrives(w, j))
        def _():
            for m in range(replicas):
                pair(w, j, m).wait_send()
                if m:
                    plane(w, j, m).wait_send()

    places = (positions + 1).astype(f32)

    def spread_of(named):
        return (places == named).astype(f32)[:, :named_rows].astype(bf16)

    def own_stage():
        for pay in pays:
            pay.wait_recv()
        named = sum(payload[m, topk : topk + 1, :] for m in range(replicas))
        spread = spread_of(named)
        rest = jnp.concatenate([payload[m, :topk, :] for m in range(replicas)], axis=0)
        summed = 0.0
        for _ in range(3):
            top = rest.astype(bf16)
            summed = summed + jnp.dot(spread, top, preferred_element_type=f32)
            rest = rest - top.astype(f32)
        new_momentum, new_params = step(momentum[...], params[...], summed / replicas)
        rounded = new_params.astype(bf16)
        picked = lax.dot_general(spread, rounded, (((0,), (0,)), ((), ())), preferred_element_type=f32)
        fixes[fsdp, :named_rows, :] = picked.astype(bf16)
        high = jnp.floor(named / 16)
        row = lax.broadcasted_iota(jnp.int32, (16, width), 0)
        digits = jnp.where(row == 0, high, jnp.where(row == 1, named - 16 * high, 0.0))
        fixes[fsdp, named_rows:, :] = digits.astype(bf16)
        fix = fixes.at[fsdp]
        for d in range(1, groups):
            fix_outs.append(go(remote(fix, fix, fix_send.at[d], fix_recv.at[d], along(d))))
        fix_siblings.append(go(remote(fix, fix, fix_core_send.at[0], fix_core_recv.at[0], sibling)))
        params_out[...] = new_params
        momentum_out[...] = new_momentum
        final[own_rows, :] = rounded

    def fix_shard(shard):
        here = pl.ds(pl.multiple_of(shard * rows, rows), rows)
        digits = fixes[shard, named_rows:, :].astype(f32)
        spread = spread_of(16 * digits[0:1, :] + digits[1:2, :])
        total = jnp.dot(spread, fixes[shard, :named_rows, :], preferred_element_type=f32)
        count = jnp.dot(spread, jnp.ones((named_rows, width // 2), bf16), preferred_element_type=f32)
        count = jnp.concatenate([count, count], axis=1)
        value = total / jnp.maximum(count, 1.0)
        final[here, :] = jnp.where(count > 0.5, value, gathered[here, :].astype(f32)).astype(bf16)

    fix_outs, fix_siblings = [], []
    for w in range(2):
        z_stage(w, 1)
    own_stage()
    for w, j in hops[2:]:
        z_stage(w, j)
    for d in range(1, groups):
        fix_outs[d - 1].wait_recv()
        fix = fixes.at[source(d) * 2 + core]
        fix_siblings.append(go(remote(fix, fix, fix_core_send.at[d], fix_core_recv.at[d], sibling)))
    for w, j in hops:
        plane_stage(w, j)
    for d in range(1, groups):
        fix_shard(source(d) * 2 + core)
    for fix in fix_siblings:
        fix.wait_recv()
    whole.wait_recv()
    fix_shard(group * 2 + 1 - core)
    for w, j in hops:
        last_stage(w, j)
    for w in range(2):
        for j in range(groups - 1):
            pl.when(goes(w, j))(hop(w, j).wait_send)
    for w, j in hops:
        drain(w, j)
    for copy in sends:
        copy.wait_send()


def write_kernel(params, momentum, error, gathered, params_out, momentum_out, error_out, gathered_out, sem):
    pairs = ((gathered, gathered_out), (params, params_out), (momentum, momentum_out), (error, error_out.at[0]))
    copies = [pltpu.make_async_copy(src, dst, sem.at[i]) for i, (src, dst) in enumerate(pairs)]
    for copy in copies:
        copy.start()
    for copy in copies:
        copy.wait()


def per_device(replicas, shards, pseudo_grad, error_buf, momentum, params, picks):
    rows, width = params.shape
    topk = picks.shape[1]
    groups = shards // 2
    f32, bf16 = jnp.float32, jnp.bfloat16
    shard = (rows, width)
    dma = pltpu.SemaphoreType.DMA
    vmem = pl.BlockSpec(memory_space=pltpu.VMEM)
    hbm = pl.BlockSpec(memory_space=pltpu.HBM)
    held = pl.pallas_call(
        functools.partial(exchange_kernel, replicas, shards, topk),
        out_shape=(
            pltpu.VMEM(shard, f32),
            pltpu.VMEM(shard, f32),
            pltpu.VMEM(shard, f32),
            pltpu.VMEM((shards * rows, width), bf16),
        ),
        in_specs=[hbm] * 5,
        out_specs=[vmem] * 4,
        scratch_shapes=[
            pltpu.SMEM((1, topk), jnp.int32),
            pltpu.VMEM(shard, f32),
            pltpu.VMEM(shard, f32),
            pltpu.VMEM(shard, f32),
            pltpu.VMEM(shard, f32),
            pltpu.VMEM((replicas, 2 * topk, width), f32),
            pltpu.VMEM((shards * rows, width), bf16),
            pltpu.VMEM((shards, replicas * topk + 16, width), bf16),
            dma((5,)),
            dma((replicas,)),
            dma((replicas,)),
            dma((2, groups)),
            dma((2, groups)),
            dma((2, groups, replicas)),
            dma((2, groups, replicas)),
            dma((2, groups, replicas)),
            dma((2, groups, replicas)),
            dma((groups,)),
            dma((groups,)),
            dma((groups,)),
            dma((groups,)),
        ],
        compiler_params=pltpu.CompilerParams(
            collective_id=0, has_side_effects=True, vmem_limit_bytes=32 * 1024 * 1024
        ),
        name="exchange",
    )(*(pltpu.with_memory_space_constraint(x, pltpu.HBM) for x in (picks, pseudo_grad, error_buf, momentum, params)))
    return pl.pallas_call(
        write_kernel,
        out_shape=(
            jax.ShapeDtypeStruct(shard, f32),
            jax.ShapeDtypeStruct(shard, f32),
            jax.ShapeDtypeStruct((1, rows, width), f32),
            jax.ShapeDtypeStruct((shards * rows, width), bf16),
        ),
        in_specs=[vmem] * 4,
        out_specs=[hbm] * 4,
        scratch_shapes=[dma((4,))],
        compiler_params=pltpu.CompilerParams(vmem_limit_bytes=16 * 1024 * 1024),
        name="write_out",
    )(*(pltpu.with_memory_space_constraint(x, pltpu.VMEM) for x in held))


def solution(mesh):
    in_specs = (
        P("rep", "fsdp", None),
        P("rep", "fsdp", None),
        P("fsdp", None),
        P("fsdp", None),
        P("rep", "fsdp"),
    )
    out_specs = (P("fsdp", None), P("fsdp", None), P("rep", "fsdp", None), P())
    step = functools.partial(per_device, mesh.shape["rep"], mesh.shape["fsdp"])
    return jax.shard_map(step, mesh=mesh, in_specs=in_specs, out_specs=out_specs, check_vma=False)
```
